32 devices in a mesh: site: 32 (over z, y, x, core).
Axes of the slice: x: 2, y: 2, z: 4, core: 2. Of those that a mesh axis runs over, the one named last changes fastest.
Arguments:
- site_tensors: bfloat16 [32, 256, 8, 256], P('site'), may hold values from -1.5 to 1.5
- first_gates: bfloat16 [32, 64, 64], P('site'), may hold values from -0.75 to 0.75
- second_gates: bfloat16 [32, 64, 64], P('site'), may hold values from -0.75 to 0.75
- first_sketch: int32 [32, 2048, 256], P('site'), may hold values from -1 to 1
- second_sketch: int32 [32, 2048, 256], P('site'), may hold values from -1 to 1
Outputs:
- evolved: bfloat16 [32, 256, 8, 256], P('site')
The draws below stay inside these ranges and needn't reach their ends.
All inputs are finite; a program needn't handle non-finite values.
Results may differ from the reference program's by a relative error of at most 0.018.
Values may be sent and summed in bfloat16 or wider, within the bound.
A program may use at most 64 MiB of HBM per device.

```python
import jax
import jax.numpy as jnp
from jax import lax

CHI = 256
LEVELS = 8
SITES = 32


def place_ends(entries, key, low, largest):
    longest = entries.shape.index(max(entries.shape))
    spots = []
    for shift in (0, 1):
        where = [jax.random.randint(jax.random.fold_in(key, axis), (), 0, length) for axis, length in enumerate(entries.shape)]
        where[longest] = (where[longest] + shift) % entries.shape[longest]
        spots.append(tuple(where))
    return entries.at[spots[0]].set(low).at[spots[1]].set(largest)


def block_scale(own_key, extent, split, smallest, high):
    def one(dim, parts):
        steps = jax.random.uniform(jax.random.fold_in(jax.random.fold_in(own_key, 6), dim), (parts,), jnp.float32, smallest / len(split), high / len(split))
        return jnp.repeat(jnp.exp(steps), extent[dim] // parts).reshape((-1,) + (1,) * (len(extent) - dim - 1))

    gain = one(*split[0])
    for cut in split[1:]:
        gain = gain * one(*cut)
    return gain


def normal_values(key, dims, scale, most, shards=(), kind=jnp.bfloat16):
    loudness = block_scale(key, dims, shards, -0.22, 0.18) if shards else 1.0
    values = jax.random.normal(key, dims, jnp.float32) * scale * loudness
    return jnp.minimum(jnp.maximum(values, -most), most).astype(kind)


def setup_inputs(seed: int = 0) -> dict:
    seeds = jax.random.split(jax.random.key(seed), 6)
    site_tensors = normal_values(seeds[0], (SITES, CHI, LEVELS, CHI), (CHI ** 0.5) ** -0.5, 1.5, ((0, 32),))
    first_gates = normal_values(seeds[1], (SITES, LEVELS * LEVELS, LEVELS * LEVELS), (LEVELS * LEVELS) ** -0.5, 0.75, ((0, 32),))
    second_gates = normal_values(seeds[2], (SITES, LEVELS * LEVELS, LEVELS * LEVELS), (LEVELS * LEVELS) ** -0.5, 0.75, ((0, 32),))
    first_sketch = place_ends(jax.random.randint(seeds[3], (SITES, LEVELS * CHI, CHI), -1, 2), jax.random.fold_in(seeds[3], 1), -1, 1).astype(jnp.int32)
    second_sketch = place_ends(jax.random.randint(seeds[4], (SITES, LEVELS * CHI, CHI), -1, 2), jax.random.fold_in(seeds[4], 1), -1, 1).astype(jnp.int32)
    return {"site_tensors": site_tensors, "first_gates": first_gates, "second_gates": second_gates, "first_sketch": first_sketch, "second_sketch": second_sketch}


def update_pair(left_tensor, right_tensor, gate_matrix, sketch_matrix):
    two_site = jnp.dot(left_tensor.reshape(CHI * LEVELS, CHI).astype(jnp.float32), right_tensor.reshape(CHI, LEVELS * CHI).astype(jnp.float32), preferred_element_type=jnp.float32).astype(jnp.bfloat16)
    two_site = two_site.reshape(CHI, LEVELS * LEVELS, CHI)
    gated_pair = jnp.einsum('xy,ayc->axc', gate_matrix.astype(jnp.float32), two_site.astype(jnp.float32)).astype(jnp.bfloat16)
    matrix = gated_pair.reshape(CHI * LEVELS, LEVELS * CHI)
    sampled = jnp.dot(matrix.astype(jnp.float32), sketch_matrix.astype(jnp.bfloat16).astype(jnp.float32), preferred_element_type=jnp.float32)
    gram_matrix = jnp.dot(sampled.T, sampled, precision=lax.Precision.HIGHEST)
    factor_lower = jnp.linalg.cholesky(gram_matrix)
    basis_rows = jax.scipy.linalg.solve_triangular(factor_lower, sampled.T, lower=True)
    new_left = (basis_rows.T * (LEVELS ** 0.5 * CHI ** 0.25)).astype(jnp.bfloat16)
    product = lax.dot_general(new_left.astype(jnp.float32), matrix.astype(jnp.float32), (((0,), (0,)), ((), ())), preferred_element_type=jnp.float32)
    new_right = (product * (LEVELS * CHI) ** (-0.5)).astype(jnp.bfloat16)
    return (new_left.reshape(CHI, LEVELS, CHI), new_right.reshape(CHI, LEVELS, CHI))

def apply_layer(tensors, gates, sketches, parity):

    def advance(pair_index, current):
        left_index = (parity + 2 * pair_index).astype(jnp.int32)
        right_index = jnp.minimum(left_index + 1, SITES - 1).astype(jnp.int32)
        inside = left_index + 1 < SITES
        left_tensor = lax.dynamic_index_in_dim(current, left_index, 0, keepdims=False)
        right_tensor = lax.dynamic_index_in_dim(current, right_index, 0, keepdims=False)
        gate_matrix = lax.dynamic_index_in_dim(gates, left_index, 0, keepdims=False)
        sketch_matrix = lax.dynamic_index_in_dim(sketches, left_index, 0, keepdims=False)
        new_left, new_right = update_pair(left_tensor, right_tensor, gate_matrix, sketch_matrix)
        new_left = jnp.where(inside, new_left, left_tensor)
        new_right = jnp.where(inside, new_right, right_tensor)
        current = lax.dynamic_update_index_in_dim(current, new_right, right_index, 0)
        current = lax.dynamic_update_index_in_dim(current, new_left, left_index, 0)
        return current
    return lax.fori_loop(0, SITES // 2, advance, tensors)

def reference(site_tensors, first_gates, second_gates, first_sketch, second_sketch):
    tensors = apply_layer(site_tensors, first_gates, first_sketch, 0)
    tensors = apply_layer(tensors, second_gates, second_sketch, 1)
    return tensors
```

```python
import functools

import jax
import jax.numpy as jnp
from jax import lax
from jax.experimental import pallas as pl
from jax.experimental.pallas import tpu as pltpu
from jax.sharding import PartitionSpec as P

PANEL = 32
F32 = jnp.float32
BF16 = jnp.bfloat16


def dot(a, b, dims=((1,), (0,)), precision=None):
    return lax.dot_general(a, b, (dims, ((), ())), precision=precision, preferred_element_type=F32)


def split(x, parts):
    pieces = []
    for _ in range(parts):
        piece = x.astype(BF16)
        pieces.append(piece)
        x = x - piece.astype(F32)
    return pieces


def wide_gate(gate, levels, group):
    size = levels * levels * group

    def pick(position):
        high, low = position // (group * levels), position % levels
        return low * levels + high

    rows = pick(lax.broadcasted_iota(jnp.int32, (size, levels * levels), 0))
    left = (rows == lax.broadcasted_iota(jnp.int32, (size, levels * levels), 1)).astype(F32).astype(BF16)
    columns = pick(lax.broadcasted_iota(jnp.int32, (levels * levels, size), 1))
    right = (columns == lax.broadcasted_iota(jnp.int32, (levels * levels, size), 0)).astype(F32).astype(BF16)
    spread = dot(dot(left, gate).astype(BF16), right)
    bond_of = lambda axis: (lax.broadcasted_iota(jnp.int32, (size, size), axis) // levels) % group
    return jnp.where(bond_of(0) == bond_of(1), spread, 0.0).astype(BF16)


def invert_factor(gram):
    size = gram.shape[0]
    work = gram
    done = []
    for start in range(0, size, PANEL):
        panel = work[:PANEL]
        rest = work[PANEL:]
        row_of = lax.broadcasted_iota(jnp.int32, (PANEL, 1), 0)
        lane_of = lax.broadcasted_iota(jnp.int32, (1, size), 1)
        for k in range(PANEL):
            lane = start + k
            column = panel[:, lane : lane + 1]
            root = lax.rsqrt(column[k : k + 1])
            row = jnp.where(lane_of == lane, 1.0, panel[k : k + 1]) * root
            below = row_of > k
            factor = jnp.where(below, column * root, 0.0)
            cleared = jnp.where(below & (lane_of == lane), 0.0, panel)
            panel = jnp.where(row_of == k, row, cleared - factor * row)
        done.append(panel)
        if start + PANEL < size:
            past = lane_of >= start + PANEL
            upper = jnp.where(past, panel, 0.0)
            inside = (lane_of >= start) & (lane_of < start + PANEL)
            reached = jnp.where(inside & (lane_of > start + row_of), 0.0, panel)
            update = dot(upper, reached, ((0,), (0,)), lax.Precision.HIGHEST)
            work = jnp.where(inside, 0.0, rest) - update[start + PANEL :]
    lower = jnp.concatenate(done, axis=0)
    keep = lax.broadcasted_iota(jnp.int32, (size, size), 0) >= lax.broadcasted_iota(jnp.int32, (size, size), 1)
    return jnp.where(keep, lower, 0.0)


def layer_kernel(
    parity, levels, bond,
    own, other, own_gate, other_gate, own_sketch, other_sketch, out,
    left, right, right_wide, spread, gate, wide, sketch, matrix, sampled, gram, basis_t, sems,
):
    devices = lax.axis_size("site")
    position = lax.axis_index("site")
    is_left = ((position - parity) % 2 == 0) & (position >= parity) & (position + 1 < devices)
    is_right = ((position - parity) % 2 != 0) & (position > parity)
    rows = bond * levels
    group = wide.shape[0] // (levels * levels)
    height = group * levels
    chunk = bond
    left_scale = levels**0.5 * bond**0.25
    right_scale = rows**-0.5

    def fetch(pairs):
        copies = [pltpu.make_async_copy(a, b, sems.at[i]) for i, (a, b) in enumerate(pairs)]
        for copy in copies:
            copy.start()
        for copy in copies:
            copy.wait()

    @pl.when(is_left)
    def _():
        fetch([(own, left), (other, right), (own_gate, gate), (own_sketch, sketch)])

    @pl.when(is_right)
    def _():
        fetch([(other, left), (own, right), (other_gate, gate), (other_sketch, sketch)])

    @pl.when(jnp.logical_not(is_left | is_right))
    def _():
        fetch([(own, out)])

    @pl.when(is_left | is_right)
    def _():
        wide[...] = wide_gate(gate[...], levels, group)
        spread[...] = right[...].astype(F32).reshape(bond, levels, bond)
        for s in range(levels):
            right_wide[:, s * bond : (s + 1) * bond] = spread[:, s, :].astype(BF16)
        gram[...] = jnp.zeros_like(gram)

        @pl.loop(0, rows // chunk)
        def _(step):
            base = pl.multiple_of(step * chunk, chunk)
            two_site = dot(left[pl.ds(base, chunk), :], right_wide[...]).astype(BF16)
            for g in range(chunk // height):
                part = two_site[g * height : (g + 1) * height]
                stacked = jnp.concatenate([part[:, s * bond : (s + 1) * bond] for s in range(levels)], axis=0)
                gated = dot(wide[...], stacked).astype(BF16)
                at = pl.multiple_of(base + g * height, height)
                for t in range(levels):
                    matrix[pl.ds(at, height), t * bond : (t + 1) * bond] = gated[t * height : (t + 1) * height]
            drawn = dot(matrix[pl.ds(base, chunk), :], sketch[...])
            sampled[pl.ds(base, chunk), :] = drawn
            high, middle, low = split(drawn, 3)
            cross = dot(high, middle, ((0,), (0,))) + dot(high, low, ((0,), (0,)))
            square = dot(high, high, ((0,), (0,))) + dot(middle, middle, ((0,), (0,)))
            gram[...] += square + (cross + cross.T)

        inverse = invert_factor(gram[...])
        inv_high, inv_low = split(inverse.T * left_scale, 2)

        def basis_at(base):
            high, low = split(sampled[pl.ds(base, chunk), :], 2)
            return dot(high, inv_high) + (dot(high, inv_low) + dot(low, inv_high))

        @pl.when(is_left)
        def _():
            for step in range(rows // chunk):
                out[step * chunk : (step + 1) * chunk, :] = basis_at(step * chunk).astype(BF16)

        @pl.when(is_right)
        def _():
            for step in range(rows // chunk):
                basis_t[:, step * chunk : (step + 1) * chunk] = basis_at(step * chunk).T.astype(BF16)
            for t in range(levels):
                product = dot(basis_t[...], matrix[:, t * bond : (t + 1) * bond])
                spread[:, t, :] = product * right_scale
            out[...] = spread[...].reshape(rows, bond).astype(BF16)


def apply_layer(parity, own, other, own_gate, other_gate, own_sketch, other_sketch):
    bond, levels = own_sketch.shape[1], own.shape[0] // own_sketch.shape[1]
    rows = bond * levels
    group = max(1, bond // (levels * levels))
    size = group * levels * levels
    return pl.pallas_call(
        functools.partial(layer_kernel, parity, levels, bond),
        out_shape=jax.ShapeDtypeStruct((rows, bond), BF16),
        in_specs=[pl.BlockSpec(memory_space=pl.ANY)] * 6,
        out_specs=pl.BlockSpec(memory_space=pltpu.VMEM),
        scratch_shapes=[
            pltpu.VMEM((rows, bond), BF16),
            pltpu.VMEM((rows, bond), BF16),
            pltpu.VMEM((bond, rows), BF16),
            pltpu.VMEM((bond, levels, bond), F32),
            pltpu.VMEM(own_gate.shape, BF16),
            pltpu.VMEM((size, size), BF16),
            pltpu.VMEM((rows, bond), BF16),
            pltpu.VMEM((rows, rows), BF16),
            pltpu.VMEM((rows, bond), F32),
            pltpu.VMEM((bond, bond), F32),
            pltpu.VMEM((bond, rows), BF16),
            pltpu.SemaphoreType.DMA((4,)),
        ],
        compiler_params=pltpu.CompilerParams(vmem_limit_bytes=48 * 1024 * 1024),
        cost_estimate=pl.CostEstimate(flops=8 * rows * rows * bond, bytes_accessed=8 * rows * bond, transcendentals=0),
    )(own, other, own_gate, other_gate, own_sketch, other_sketch)


def per_device(site_tensors, first_gates, second_gates, first_sketch, second_sketch):
    size = lax.axis_size("site")
    _, bond, levels, _ = site_tensors.shape
    tensor = site_tensors.reshape(bond * levels, bond)
    arguments = [
        (0, first_gates[0], first_sketch[0].astype(BF16)),
        (1, second_gates[0], second_sketch[0].astype(BF16)),
    ]
    sent = []
    for parity, gate, sketch in arguments:
        to_right = [(i, i + 1) for i in range(parity, size - 1, 2)]
        sent.append((lax.ppermute(gate, "site", to_right), lax.ppermute(sketch, "site", to_right)))
    for (parity, gate, sketch), (other_gate, other_sketch) in zip(arguments, sent):
        swaps = [pair for i in range(parity, size - 1, 2) for pair in ((i, i + 1), (i + 1, i))]
        other = lax.ppermute(tensor, "site", swaps)
        tensor = apply_layer(parity, tensor, other, gate, other_gate, sketch, other_sketch)
    return tensor.reshape(site_tensors.shape)


def solution(mesh):
    in_specs = (
        P("site", None, None, None),
        P("site", None, None),
        P("site", None, None),
        P("site", None, None),
        P("site", None, None),
    )
    out_specs = P("site", None, None, None)
    return jax.shard_map(
        per_device, mesh=mesh, in_specs=in_specs, out_specs=out_specs, check_vma=False
    )
```

```python
import functools

import jax
import jax.numpy as jnp
from jax import lax
from jax.experimental import pallas as pl
from jax.experimental.pallas import tpu as pltpu
from jax.sharding import PartitionSpec as P

PANEL = 32
TILE = 8
F32 = jnp.float32
BF16 = jnp.bfloat16


def dot(a, b, dims=((1,), (0,)), precision=None):
    return lax.dot_general(a, b, (dims, ((), ())), precision=precision, preferred_element_type=F32)


def split(x, parts):
    pieces = []
    for _ in range(parts):
        piece = x.astype(BF16)
        pieces.append(piece)
        x = x - piece.astype(F32)
    return pieces


def wide_gate(gate, levels, group):
    size = levels * levels * group

    def pick(position):
        high, low = position // (group * levels), position % levels
        return low * levels + high

    rows = pick(lax.broadcasted_iota(jnp.int32, (size, levels * levels), 0))
    left = (rows == lax.broadcasted_iota(jnp.int32, (size, levels * levels), 1)).astype(F32).astype(BF16)
    columns = pick(lax.broadcasted_iota(jnp.int32, (levels * levels, size), 1))
    right = (columns == lax.broadcasted_iota(jnp.int32, (levels * levels, size), 0)).astype(F32).astype(BF16)
    spread = dot(dot(left, gate).astype(BF16), right)
    bond_of = lambda axis: (lax.broadcasted_iota(jnp.int32, (size, size), axis) // levels) % group
    return jnp.where(bond_of(0) == bond_of(1), spread, 0.0).astype(BF16)


def eliminate_tile(tiles, first, lane, lane_of):
    size = tiles[first].shape[1]
    width = min(size, 128)
    shape = (TILE, width)
    columns = [
        [jnp.broadcast_to(tile[:, lane + j : lane + j + 1], shape) for j in range(TILE)] for tile in tiles[first:]
    ]
    pivot = columns[0]
    entry = {(i, j): jnp.broadcast_to(pivot[j][i : i + 1], shape) for j in range(TILE) for i in range(j, TILE)}
    here = (lane_of >= lane) & (lane_of < lane + TILE)
    rows = []
    for j in range(TILE):
        row = jnp.broadcast_to(tiles[first][j : j + 1], (TILE, size))
        rows.append(jnp.where(here, jnp.where(lane_of == lane + j, 1.0, 0.0), row))
    repeat = lambda x: jnp.concatenate([x] * (size // width), axis=1)
    for j in range(TILE):
        root = lax.rsqrt(entry[j, j])
        for i in range(j + 1, TILE):
            entry[i, j] = entry[i, j] * root
        for m in range(j + 1, TILE):
            for i in range(m, TILE):
                entry[i, m] = entry[i, m] - entry[i, j] * entry[m, j]
        rows[j] = rows[j] * repeat(root)
        for below in columns[1:]:
            below[j] = below[j] * root
        for m in range(j + 1, TILE):
            rows[m] = rows[m] - repeat(entry[m, j]) * rows[j]
            for below in columns[1:]:
                below[m] = below[m] - entry[m, j] * below[j]
    row_of = lax.broadcasted_iota(jnp.int32, (TILE, 1), 0)
    whole = rows[0]
    for j in range(1, TILE):
        whole = jnp.where(row_of == j, rows[j], whole)
    result = tiles[:first] + [whole]
    for tile, below in zip(tiles[first + 1 :], columns[1:]):
        terms = [repeat(below[j]) * rows[j] for j in range(TILE)]
        while len(terms) > 1:
            terms = [a + b for a, b in zip(terms[::2], terms[1::2])]
        result.append(jnp.where(here, 0.0, tile) - terms[0])
    return result


def invert_factor(gram):
    size = gram.shape[0]
    work = gram
    done = []
    row_of = lax.broadcasted_iota(jnp.int32, (PANEL, 1), 0)
    lane_of = lax.broadcasted_iota(jnp.int32, (1, size), 1)
    for start in range(0, size, PANEL):
        tiles = [work[i : i + TILE] for i in range(0, PANEL, TILE)]
        for first in range(PANEL // TILE):
            tiles = eliminate_tile(tiles, first, start + first * TILE, lane_of)
        panel = jnp.concatenate(tiles, axis=0)
        done.append(panel)
        if start + PANEL < size:
            upper = jnp.where(lane_of >= start + PANEL, panel, 0.0)
            inside = (lane_of >= start) & (lane_of < start + PANEL)
            reached = jnp.where(inside & (lane_of > start + row_of), 0.0, panel)
            update = dot(upper, reached, ((0,), (0,)), lax.Precision.HIGHEST)
            work = jnp.where(inside, 0.0, work[PANEL:]) - update[start + PANEL :]
    lower = jnp.concatenate(done, axis=0)
    keep = lax.broadcasted_iota(jnp.int32, (size, size), 0) >= lax.broadcasted_iota(jnp.int32, (size, size), 1)
    return jnp.where(keep, lower, 0.0)


def layer_kernel(
    parity, levels, bond,
    own, other, own_packed, other_packed, out,
    left, right, right_wide, spread, gate, wide, sketch, matrix, sampled, gram, basis_t, sems,
):
    devices = lax.axis_size("site")
    position = lax.axis_index("site")
    is_left = ((position - parity) % 2 == 0) & (position >= parity) & (position + 1 < devices)
    is_right = ((position - parity) % 2 != 0) & (position > parity)
    rows = bond * levels
    group = wide.shape[0] // (levels * levels)
    height = group * levels
    chunk = bond
    left_scale = levels**0.5 * bond**0.25
    right_scale = rows**-0.5

    def fetch(pairs):
        copies = [pltpu.make_async_copy(a, b, sems.at[i]) for i, (a, b) in enumerate(pairs)]
        for copy in copies:
            copy.start()
        for copy in copies:
            copy.wait()

    def unpack(packed):
        return [(packed.at[0:rows], sketch), (packed.at[rows : rows + gate.shape[0]], gate)]

    @pl.when(is_left)
    def _():
        fetch([(own, left), (other, right)] + unpack(own_packed))

    @pl.when(is_right)
    def _():
        fetch([(other, left), (own, right)] + unpack(other_packed))

    @pl.when(jnp.logical_not(is_left | is_right))
    def _():
        fetch([(own, out)])

    @pl.when(is_left | is_right)
    def _():
        wide[...] = wide_gate(gate[:, : levels * levels], levels, group)
        spread[...] = right[...].astype(F32).reshape(bond, levels, bond)
        for s in range(levels):
            right_wide[:, s * bond : (s + 1) * bond] = spread[:, s, :].astype(BF16)
        gram[...] = jnp.zeros_like(gram)

        @pl.loop(0, rows // chunk)
        def _(step):
            base = pl.multiple_of(step * chunk, chunk)
            two_site = dot(left[pl.ds(base, chunk), :], right_wide[...]).astype(BF16)
            for g in range(chunk // height):
                part = two_site[g * height : (g + 1) * height]
                stacked = jnp.concatenate([part[:, s * bond : (s + 1) * bond] for s in range(levels)], axis=0)
                gated = dot(wide[...], stacked).astype(BF16)
                at = pl.multiple_of(base + g * height, height)
                for t in range(levels):
                    matrix[pl.ds(at, height), t * bond : (t + 1) * bond] = gated[t * height : (t + 1) * height]
            drawn = dot(matrix[pl.ds(base, chunk), :], sketch[...])
            sampled[pl.ds(base, chunk), :] = drawn
            high, middle, low = split(drawn, 3)
            cross = dot(high, middle, ((0,), (0,))) + dot(high, low, ((0,), (0,)))
            square = dot(high, high, ((0,), (0,))) + dot(middle, middle, ((0,), (0,)))
            gram[...] += square + (cross + cross.T)

        inverse = invert_factor(gram[...])
        inv_high, inv_low = split(inverse.T * left_scale, 2)

        def basis_at(base):
            high, low = split(sampled[pl.ds(base, chunk), :], 2)
            return dot(high, inv_high) + (dot(high, inv_low) + dot(low, inv_high))

        @pl.when(is_left)
        def _():
            for step in range(rows // chunk):
                out[step * chunk : (step + 1) * chunk, :] = basis_at(step * chunk).astype(BF16)

        @pl.when(is_right)
        def _():
            for step in range(rows // chunk):
                basis_t[:, step * chunk : (step + 1) * chunk] = basis_at(step * chunk).T.astype(BF16)
            for t in range(levels):
                product = dot(basis_t[...], matrix[:, t * bond : (t + 1) * bond])
                spread[:, t, :] = product * right_scale
            out[...] = spread[...].reshape(rows, bond).astype(BF16)


def apply_layer(parity, own, other, own_packed, other_packed):
    bond, levels = own.shape[1], own.shape[0] // own.shape[1]
    rows = bond * levels
    group = max(1, bond // (levels * levels))
    size = group * levels * levels
    return pl.pallas_call(
        functools.partial(layer_kernel, parity, levels, bond),
        out_shape=jax.ShapeDtypeStruct((rows, bond), BF16),
        in_specs=[pl.BlockSpec(memory_space=pl.ANY)] * 4,
        out_specs=pl.BlockSpec(memory_space=pltpu.VMEM),
        scratch_shapes=[
            pltpu.VMEM((rows, bond), BF16),
            pltpu.VMEM((rows, bond), BF16),
            pltpu.VMEM((bond, rows), BF16),
            pltpu.VMEM((bond, levels, bond), F32),
            pltpu.VMEM((levels * levels, bond), BF16),
            pltpu.VMEM((size, size), BF16),
            pltpu.VMEM((rows, bond), BF16),
            pltpu.VMEM((rows, rows), BF16),
            pltpu.VMEM((rows, bond), F32),
            pltpu.VMEM((bond, bond), F32),
            pltpu.VMEM((bond, rows), BF16),
            pltpu.SemaphoreType.DMA((4,)),
        ],
        compiler_params=pltpu.CompilerParams(vmem_limit_bytes=48 * 1024 * 1024),
        cost_estimate=pl.CostEstimate(flops=8 * rows * rows * bond, bytes_accessed=8 * rows * bond, transcendentals=0),
    )(own, other, own_packed, other_packed)


def per_device(site_tensors, first_gates, second_gates, first_sketch, second_sketch):
    size = lax.axis_size("site")
    _, bond, levels, _ = site_tensors.shape
    tensor = site_tensors.reshape(bond * levels, bond)
    packs = []
    for gate, sketch in ((first_gates[0], first_sketch[0]), (second_gates[0], second_sketch[0])):
        padded = jnp.pad(gate, ((0, 0), (0, bond - gate.shape[1])))
        packs.append(jnp.concatenate([sketch.astype(BF16), padded], axis=0))
    sent = []
    for parity, packed in enumerate(packs):
        to_right = [(i, i + 1) for i in range(parity, size - 1, 2)]
        sent.append(lax.ppermute(packed, "site", to_right))
    for parity, packed in enumerate(packs):
        swaps = [pair for i in range(parity, size - 1, 2) for pair in ((i, i + 1), (i + 1, i))]
        other = lax.ppermute(tensor, "site", swaps)
        tensor = apply_layer(parity, tensor, other, packed, sent[parity])
    return tensor.reshape(site_tensors.shape)


def solution(mesh):
    in_specs = (
        P("site", None, None, None),
        P("site", None, None),
        P("site", None, None),
        P("site", None, None),
        P("site", None, None),
    )
    out_specs = P("site", None, None, None)
    return jax.shard_map(
        per_device, mesh=mesh, in_specs=in_specs, out_specs=out_specs, check_vma=False
    )
```

```python
import functools

import jax
import jax.numpy as jnp
from jax import lax
from jax.experimental import pallas as pl
from jax.experimental.pallas import tpu as pltpu
from jax.sharding import PartitionSpec as P

PANEL = 64
TILE = 8
F32 = jnp.float32
BF16 = jnp.bfloat16


def dot(a, b, dims=((1,), (0,)), precision=None):
    return lax.dot_general(a, b, (dims, ((), ())), precision=precision, preferred_element_type=F32)


def split(x, parts):
    pieces = []
    for _ in range(parts):
        piece = x.astype(BF16)
        pieces.append(piece)
        x = x - piece.astype(F32)
    return pieces


def wide_gate(gate, levels, group):
    size = levels * levels * group

    def pick(position):
        high, low = position // (group * levels), position % levels
        return low * levels + high

    rows = pick(lax.broadcasted_iota(jnp.int32, (size, levels * levels), 0))
    left = (rows == lax.broadcasted_iota(jnp.int32, (size, levels * levels), 1)).astype(F32).astype(BF16)
    columns = pick(lax.broadcasted_iota(jnp.int32, (levels * levels, size), 1))
    right = (columns == lax.broadcasted_iota(jnp.int32, (levels * levels, size), 0)).astype(F32).astype(BF16)
    spread = dot(dot(left, gate).astype(BF16), right)
    bond_of = lambda axis: (lax.broadcasted_iota(jnp.int32, (size, size), axis) // levels) % group
    return jnp.where(bond_of(0) == bond_of(1), spread, 0.0).astype(BF16)


def eliminate_tile(tiles, first, lane, lane_of):
    size = tiles[first].shape[1]
    width = min(size, 128)
    shape = (TILE, width)
    columns = [
        [jnp.broadcast_to(tile[:, lane + j : lane + j + 1], shape) for j in range(TILE)] for tile in tiles[first:]
    ]
    pivot = columns[0]
    entry = {(i, j): jnp.broadcast_to(pivot[j][i : i + 1], shape) for j in range(TILE) for i in range(j, TILE)}
    here = (lane_of >= lane) & (lane_of < lane + TILE)
    rows = []
    for j in range(TILE):
        row = jnp.broadcast_to(tiles[first][j : j + 1], (TILE, size))
        rows.append(jnp.where(here, jnp.where(lane_of == lane + j, 1.0, 0.0), row))
    repeat = lambda x: jnp.concatenate([x] * (size // width), axis=1)
    for j in range(TILE):
        root = lax.rsqrt(entry[j, j])
        for i in range(j + 1, TILE):
            entry[i, j] = entry[i, j] * root
        for m in range(j + 1, TILE):
            for i in range(m, TILE):
                entry[i, m] = entry[i, m] - entry[i, j] * entry[m, j]
        rows[j] = rows[j] * repeat(root)
        for below in columns[1:]:
            below[j] = below[j] * root
        for m in range(j + 1, TILE):
            rows[m] = rows[m] - repeat(entry[m, j]) * rows[j]
            for below in columns[1:]:
                below[m] = below[m] - entry[m, j] * below[j]
    row_of = lax.broadcasted_iota(jnp.int32, (TILE, 1), 0)
    whole = rows[0]
    for j in range(1, TILE):
        whole = jnp.where(row_of == j, rows[j], whole)
    result = tiles[:first] + [whole]
    for tile, below in zip(tiles[first + 1 :], columns[1:]):
        terms = [repeat(below[j]) * rows[j] for j in range(TILE)]
        while len(terms) > 1:
            terms = [a + b for a, b in zip(terms[::2], terms[1::2])]
        result.append(jnp.where(here, 0.0, tile) - terms[0])
    return result


def invert_factor(gram):
    size = gram.shape[0]
    work = gram
    done = []
    row_of = lax.broadcasted_iota(jnp.int32, (PANEL, 1), 0)
    lane_of = lax.broadcasted_iota(jnp.int32, (1, size), 1)
    for start in range(0, size, PANEL):
        tiles = [work[i : i + TILE] for i in range(0, PANEL, TILE)]
        for first in range(PANEL // TILE):
            tiles = eliminate_tile(tiles, first, start + first * TILE, lane_of)
        panel = jnp.concatenate(tiles, axis=0)
        done.append(panel)
        if start + PANEL < size:
            upper = jnp.where(lane_of >= start + PANEL, panel, 0.0)
            inside = (lane_of >= start) & (lane_of < start + PANEL)
            reached = jnp.where(inside & (lane_of > start + row_of), 0.0, panel)
            skip = (start + PANEL) // 128 * 128
            update = dot(upper[:, skip:], reached, ((0,), (0,)), lax.Precision.HIGHEST)
            work = jnp.where(inside, 0.0, work[PANEL:]) - update[start + PANEL - skip :]
    lower = jnp.concatenate(done, axis=0)
    keep = lax.broadcasted_iota(jnp.int32, (size, size), 0) >= lax.broadcasted_iota(jnp.int32, (size, size), 1)
    return jnp.where(keep, lower, 0.0)


def layer_kernel(
    parity, levels, bond,
    own, other, own_packed, other_packed, out,
    left, right, right_wide, spread, gate, wide, sketch, matrix, sampled, gram, basis_t, sems,
):
    devices = lax.axis_size("site")
    position = lax.axis_index("site")
    is_left = ((position - parity) % 2 == 0) & (position >= parity) & (position + 1 < devices)
    is_right = ((position - parity) % 2 != 0) & (position > parity)
    rows = bond * levels
    group = wide.shape[0] // (levels * levels)
    height = group * levels
    chunk = bond
    left_scale = levels**0.5 * bond**0.25
    right_scale = rows**-0.5

    def fetch(pairs):
        copies = [pltpu.make_async_copy(a, b, sems.at[i]) for i, (a, b) in enumerate(pairs)]
        for copy in copies:
            copy.start()
        for copy in copies:
            copy.wait()

    def unpack(packed):
        return [(packed.at[0:rows], sketch), (packed.at[rows : rows + gate.shape[0]], gate)]

    @pl.when(is_left)
    def _():
        fetch([(own, left), (other, right)] + unpack(own_packed))

    @pl.when(is_right)
    def _():
        fetch([(other, left), (own, right)] + unpack(other_packed))

    @pl.when(jnp.logical_not(is_left | is_right))
    def _():
        fetch([(own, out)])

    @pl.when(is_left | is_right)
    def _():
        wide[...] = wide_gate(gate[:, : levels * levels], levels, group)
        spread[...] = right[...].astype(F32).reshape(bond, levels, bond)
        for s in range(levels):
            right_wide[:, s * bond : (s + 1) * bond] = spread[:, s, :].astype(BF16)
        gram[...] = jnp.zeros_like(gram)

        @pl.loop(0, rows // chunk)
        def _(step):
            base = pl.multiple_of(step * chunk, chunk)
            two_site = dot(left[pl.ds(base, chunk), :], right_wide[...]).astype(BF16)
            for g in range(chunk // height):
                part = two_site[g * height : (g + 1) * height]
                stacked = jnp.concatenate([part[:, s * bond : (s + 1) * bond] for s in range(levels)], axis=0)
                gated = dot(wide[...], stacked).astype(BF16)
                at = pl.multiple_of(base + g * height, height)
                for t in range(levels):
                    matrix[pl.ds(at, height), t * bond : (t + 1) * bond] = gated[t * height : (t + 1) * height]
            drawn = dot(matrix[pl.ds(base, chunk), :], sketch[...])
            sampled[pl.ds(base, chunk), :] = drawn
            high, middle, low = split(drawn, 3)
            cross = dot(high, middle, ((0,), (0,))) + dot(high, low, ((0,), (0,)))
            square = dot(high, high, ((0,), (0,))) + dot(middle, middle, ((0,), (0,)))
            gram[...] += square + (cross + cross.T)

        inverse = invert_factor(gram[...])
        inv_high, inv_low = split(inverse.T * left_scale, 2)

        def basis_at(base):
            high, low = split(sampled[pl.ds(base, chunk), :], 2)
            return dot(high, inv_high) + (dot(high, inv_low) + dot(low, inv_high))

        @pl.when(is_left)
        def _():
            for step in range(rows // chunk):
                out[step * chunk : (step + 1) * chunk, :] = basis_at(step * chunk).astype(BF16)

        @pl.when(is_right)
        def _():
            for step in range(rows // chunk):
                basis_t[:, step * chunk : (step + 1) * chunk] = basis_at(step * chunk).T.astype(BF16)
            for t in range(levels):
                product = dot(basis_t[...], matrix[:, t * bond : (t + 1) * bond])
                spread[:, t, :] = product * right_scale
            out[...] = spread[...].reshape(rows, bond).astype(BF16)


def apply_layer(parity, own, other, own_packed, other_packed):
    bond, levels = own.shape[1], own.shape[0] // own.shape[1]
    rows = bond * levels
    group = max(1, bond // (levels * levels))
    size = group * levels * levels
    return pl.pallas_call(
        functools.partial(layer_kernel, parity, levels, bond),
        out_shape=jax.ShapeDtypeStruct((rows, bond), BF16),
        in_specs=[pl.BlockSpec(memory_space=pl.ANY)] * 4,
        out_specs=pl.BlockSpec(memory_space=pltpu.VMEM),
        scratch_shapes=[
            pltpu.VMEM((rows, bond), BF16),
            pltpu.VMEM((rows, bond), BF16),
            pltpu.VMEM((bond, rows), BF16),
            pltpu.VMEM((bond, levels, bond), F32),
            pltpu.VMEM((levels * levels, bond), BF16),
            pltpu.VMEM((size, size), BF16),
            pltpu.VMEM((rows, bond), BF16),
            pltpu.VMEM((rows, rows), BF16),
            pltpu.VMEM((rows, bond), F32),
            pltpu.VMEM((bond, bond), F32),
            pltpu.VMEM((bond, rows), BF16),
            pltpu.SemaphoreType.DMA((4,)),
        ],
        compiler_params=pltpu.CompilerParams(vmem_limit_bytes=48 * 1024 * 1024),
        cost_estimate=pl.CostEstimate(flops=8 * rows * rows * bond, bytes_accessed=8 * rows * bond, transcendentals=0),
    )(own, other, own_packed, other_packed)


def per_device(site_tensors, first_gates, second_gates, first_sketch, second_sketch):
    size = lax.axis_size("site")
    _, bond, levels, _ = site_tensors.shape
    tensor = site_tensors.reshape(bond * levels, bond)
    packs = []
    for gate, sketch in ((first_gates[0], first_sketch[0]), (second_gates[0], second_sketch[0])):
        padded = jnp.pad(gate, ((0, 0), (0, bond - gate.shape[1])))
        packs.append(jnp.concatenate([sketch.astype(BF16), padded], axis=0))
    sent = []
    for parity, packed in enumerate(packs):
        to_right = [(i, i + 1) for i in range(parity, size - 1, 2)]
        sent.append(lax.ppermute(packed, "site", to_right))
    for parity, packed in enumerate(packs):
        swaps = [pair for i in range(parity, size - 1, 2) for pair in ((i, i + 1), (i + 1, i))]
        other = lax.ppermute(tensor, "site", swaps)
        tensor = apply_layer(parity, tensor, other, packed, sent[parity])
    return tensor.reshape(site_tensors.shape)


def solution(mesh):
    in_specs = (
        P("site", None, None, None),
        P("site", None, None),
        P("site", None, None),
        P("site", None, None),
        P("site", None, None),
    )
    out_specs = P("site", None, None, None)
    return jax.shard_map(
        per_device, mesh=mesh, in_specs=in_specs, out_specs=out_specs, check_vma=False
    )
```
